32 devices in a mesh: bead: 4 (over y, x), wave: 4 (over z), grp: 2 (over core).
Axes of the slice: x: 2, y: 2, z: 4, core: 2. Of those that a mesh axis runs over, the one named last changes fastest.
Arguments:
- features: float32 [4096, 512], P(('bead', 'wave', 'grp')), may hold values from -6 to 6
- positions: float32 [3, 4096], P(None, ('bead', 'wave', 'grp')), may hold values from 0 to 1
- wavevectors: int32 [3, 4096], P(None, ('wave', 'grp')), may hold values from -6 to 6
- neighbour_slots: int32 [32, 4096], P(None, ('bead', 'wave', 'grp')), may hold values from 0 to 383
- neighbour_count: int32 [4096], P(('bead', 'wave', 'grp')), may hold values from 8 to 32
- pair_distance: float32 [32, 4096], P(None, ('bead', 'wave', 'grp')), may hold values from 0.3 to 2.4
- w_self: float32 [512, 512], replicated, may hold values from -0.25 to 0.25
- w_neighbour: float32 [512, 512], replicated, may hold values from -0.25 to 0.25
- w_edge: float32 [16, 512], replicated, may hold values from -1.5 to 1.5
- w_message: float32 [512, 512], replicated, may hold values from -0.25 to 0.25
- spec_filter: float32 [4096, 512], P(('wave', 'grp')), may hold values from -4 to 4
- norm_gain: float32 [512], replicated, may hold values from 0.5 to 1.5
- w_up: float32 [512, 512], replicated, may hold values from -0.25 to 0.25
- w_down: float32 [512, 512], replicated, may hold values from -0.25 to 0.25
Outputs:
- updated: float32 [4096, 512], P(('bead', 'wave', 'grp'))
The draws below stay inside these ranges and needn't reach their ends.
All inputs are finite; a program needn't handle non-finite values.
Results may differ from the reference program's by a relative error of at most 0.0003.
Values sent between devices are 32-bit elements; how exact they have to be, the bound alone decides.
A program may use at most 128 MiB of HBM per device.

```python
import jax
import jax.numpy as jnp
from jax import lax

D = 512
KVEC = 4096
RBF = 16
KNB = 32
BLOCK = 128
BEADS = 4096


def place_ends(drawn, rng, smallest, top_value):
    index_at = [jax.random.randint(jax.random.fold_in(rng, axis), (), 0, length) for axis, length in enumerate(drawn.shape)]
    main_axis = drawn.shape.index(max(drawn.shape))
    beside = index_at[:main_axis] + [(index_at[main_axis] + 1) % drawn.shape[main_axis]] + index_at[main_axis + 1:]
    return drawn.at[tuple(index_at)].set(smallest).at[tuple(beside)].set(top_value)


def steps_of(own_key, extent, shards, low, high):
    loudness = 1.0
    for position, blocks in shards:
        heights = jax.random.uniform(jax.random.fold_in(jax.random.fold_in(own_key, 6), position), (blocks,), jnp.float32, low / len(shards), high / len(shards))
        loudness = loudness * jnp.repeat(jnp.exp(heights), extent[position] // blocks).reshape((-1,) + (1,) * (len(extent) - 1 - position))
    return loudness


def bell_draw(key, dims, scale, most, split=(), held_as=jnp.bfloat16):
    values = jax.random.normal(key, dims, jnp.float32) * scale
    if len(split) > 0:
        values = steps_of(key, dims, split, -0.22, 0.18) * values
    return jnp.clip(values, min=-most, max=most).astype(held_as)


def setup_inputs(seed: int = 0) -> dict:
    key_list = jax.random.split(jax.random.key(seed), 15)
    features = bell_draw(key_list[0], (BEADS, D), 1.0, 6.0, ((0, 32),), jnp.float32)
    positions = jnp.clip(1.0 * jax.random.uniform(key_list[1], (3, BEADS), jnp.float32) ** steps_of(key_list[1], (3, BEADS), ((1, 32),), -0.2, 0.2), 0.0, 1.0)
    wavevectors = place_ends(jax.random.randint(key_list[2], (3, KVEC), -6, 7), jax.random.fold_in(key_list[2], 1), -6, 6).astype(jnp.int32)
    neighbour_slots = place_ends(jax.random.randint(key_list[3], (KNB, BEADS), 0, 3 * BLOCK), jax.random.fold_in(key_list[3], 1), 0, (3 * BLOCK) - 1).astype(jnp.int32)
    neighbour_count = place_ends(jax.random.randint(key_list[4], (BEADS,), KNB // 4, KNB + 1), jax.random.fold_in(key_list[4], 1), KNB // 4, KNB).astype(jnp.int32)
    pair_distance = jnp.clip(0.3 + 2.1000001 * jax.random.uniform(key_list[5], (KNB, BEADS), jnp.float32) ** steps_of(key_list[5], (KNB, BEADS), ((1, 32),), -0.2, 0.2), 0.3, 2.4)
    w_self = bell_draw(key_list[6], (D, D), D ** -0.5, 0.25, (), jnp.float32)
    w_neighbour = bell_draw(key_list[7], (D, D), D ** -0.5, 0.25, (), jnp.float32)
    w_edge = bell_draw(key_list[8], (RBF, D), RBF ** -0.5, 1.5, (), jnp.float32)
    w_message = bell_draw(key_list[9], (D, D), D ** -0.5, 0.25, (), jnp.float32)
    spec_filter = bell_draw(key_list[10], (KVEC, D), 1.0, 4.0, ((0, 8),), jnp.float32)
    norm_gain = jnp.clip(1.0 + 0.1 * jax.random.normal(key_list[11], (D,), jnp.float32), 0.5, 1.5)
    w_up = bell_draw(key_list[12], (D, D), D ** -0.5, 0.25, (), jnp.float32)
    w_down = bell_draw(key_list[13], (D, D), D ** -0.5, 0.25, (), jnp.float32)
    return dict(features=features, positions=positions, wavevectors=wavevectors, neighbour_slots=neighbour_slots, neighbour_count=neighbour_count, pair_distance=pair_distance, w_self=w_self, w_neighbour=w_neighbour, w_edge=w_edge, w_message=w_message, spec_filter=spec_filter, norm_gain=norm_gain, w_up=w_up, w_down=w_down)


highest = lax.Precision.HIGHEST
epsilon = 1e-05
reach = 2.5
two_pi = 6.283185307179586

def matmul(left, right):
    return jnp.dot(left, right, precision=highest, preferred_element_type=jnp.float32)

def short_rows(self_proj, window, slot_index, count, distance, w_edge, w_message):
    slots, rows = slot_index.shape
    width = window.shape[1]
    picked = jnp.take(window, slot_index.reshape(-1), axis=0).reshape(slots, rows, width)
    radial = w_edge.shape[0]
    spacing = reach / (radial - 1)
    centers = jnp.arange(radial, dtype=jnp.float32) * spacing
    basis = jnp.exp(-jnp.square((distance[:, :, None] - centers) / spacing))
    edge = matmul(basis.reshape(slots * rows, radial), w_edge).reshape(slots, rows, width)
    message = jax.nn.silu(self_proj[None] + picked + edge)
    valid = (jnp.arange(slots, dtype=jnp.int32)[:, None] < count[None, :]).astype(jnp.float32)
    summed = lax.optimization_barrier(jnp.sum(message * valid[:, :, None], axis=0)) / slots
    return matmul(summed, w_message)

def phase_table(coords, vectors):
    angle = coords[0][:, None] * vectors[0][None, :] + coords[1][:, None] * vectors[1][None, :]
    angle = angle + coords[2][:, None] * vectors[2][None, :]
    angle = two_pi * angle
    return (jnp.cos(angle), jnp.sin(angle))

def reference(features, positions, wavevectors, neighbour_slots, neighbour_count, pair_distance, w_self, w_neighbour, w_edge, w_message, spec_filter, norm_gain, w_up, w_down):
    beads, width = features.shape
    nblocks = beads // BLOCK
    self_proj = matmul(features, w_self)
    neighbour_proj = matmul(features, w_neighbour)
    padded = jnp.pad(neighbour_proj, ((BLOCK, BLOCK), (0, 0)))

    def one_block(block):
        start = (block * BLOCK).astype(jnp.int32)
        own = lax.dynamic_slice_in_dim(self_proj, start, BLOCK, 0)
        window = lax.dynamic_slice_in_dim(padded, start, 3 * BLOCK, 0)
        slot_index = lax.dynamic_slice_in_dim(neighbour_slots, start, BLOCK, 1)
        count = lax.dynamic_slice_in_dim(neighbour_count, start, BLOCK, 0)
        distance = lax.dynamic_slice_in_dim(pair_distance, start, BLOCK, 1)
        return short_rows(own, window, slot_index, count, distance, w_edge, w_message)
    short = lax.map(one_block, jnp.arange(nblocks, dtype=jnp.int32)).reshape(beads, width)
    kblock = min(KVEC, 512)
    nk = KVEC // kblock
    vec_blocks = wavevectors.astype(jnp.float32).reshape(3, nk, kblock).transpose(1, 0, 2)

    def forward(vectors):
        cosine, sine = phase_table(positions, vectors)
        cos_part = jnp.einsum('nk,nd->kd', cosine, features, precision=highest)
        sin_part = jnp.einsum('nk,nd->kd', sine, features, precision=highest)
        return (cos_part, sin_part)
    cos_factor, sin_factor = lax.map(forward, vec_blocks)
    power = lax.optimization_barrier(jnp.sum(jnp.square(cos_factor) + jnp.square(sin_factor), axis=(0, 1)))
    scale = lax.rsqrt(power / (2 * KVEC) + epsilon)
    filt_blocks = spec_filter.reshape(nk, kblock, width)
    filt_cos = filt_blocks * cos_factor * scale
    filt_sin = filt_blocks * sin_factor * scale

    def inverse(carry, item):
        vectors, fc, fs = item
        cosine, sine = phase_table(positions, vectors)
        return (carry + matmul(cosine, fc) + matmul(sine, fs), None)
    long_sum, unused = lax.scan(inverse, jnp.zeros((beads, width), jnp.float32), (vec_blocks, filt_cos, filt_sin))
    long_range = long_sum / jnp.sqrt(jnp.float32(KVEC))
    total = features + short + long_range
    normed = total * lax.rsqrt(lax.optimization_barrier(jnp.mean(jnp.square(total), axis=1, keepdims=True)) + epsilon) * norm_gain
    return total + matmul(jax.nn.silu(matmul(normed, w_up)), w_down)
```

```python
import functools

import jax
import jax.numpy as jnp
from jax import lax
from jax.experimental import pallas as pl
from jax.experimental.pallas import tpu as pltpu
from jax.sharding import PartitionSpec as P

MESH = pl.DeviceIdType.MESH
F32, BF16 = jnp.float32, jnp.bfloat16
BLOCK = 128
TOP = 6
HALF = TOP + 1
TAB = 8
REACH = 2.5
EPS = 1e-05
TWO_PI = 6.283185307179586
GROUP = 4
SLOTS = 4


def split(x):
    hi = x.astype(BF16)
    return hi, (x - hi.astype(F32)).astype(BF16)


def dot(a, b, ca=1, cb=0):
    return lax.dot_general(a, b, (((ca,), (cb,)), ((), ())), preferred_element_type=F32)


def mm3(a, b, ca=1, cb=0):
    return dot(a[0], b[0], ca, cb) + (dot(a[0], b[1], ca, cb) + dot(a[1], b[0], ca, cb))


def body(
    sizes,
    feat_ref, pos_ref, spack_ref, slot_ref, count_ref, dist_ref,
    wself_ref, wneigh_ref, wedge_ref, wmsg_ref, gain_ref, wup_ref, wdown_ref,
    out_ref,
    pack, fall, spall, halo, xyh, xyl, ztab, ytab, ah, al, tacc, lng, back, lt,
    wt, selft, acc, gacc,
    fs, fr, ss, sr, hs, hr, bs, br,
):
    nb, nw, ng = sizes
    n, nj = nb * nw * ng, nw * ng
    rows, width = feat_ref.shape
    fpd = width // n
    fp = max(fpd, 16)
    cf = TAB * fp
    ch = GROUP * BLOCK
    nq = n // GROUP
    kloc = spack_ref.shape[2]
    ib, iw, ig = lax.axis_index("bead"), lax.axis_index("wave"), lax.axis_index("grp")
    mine = iw * ng + ig
    me = ib * nj + mine

    def coords(p):
        return (lax.div(p, nj), lax.rem(lax.div(p, ng), nw), lax.rem(p, ng))

    barrier = pltpu.get_barrier_semaphore()

    def greet(t, _):
        pl.semaphore_signal(barrier, inc=1, device_id=coords(lax.rem(me + t, n)), device_id_type=MESH)
        return 0

    lax.fori_loop(1, n, greet, 0)

    ft = feat_ref[...].T
    angle = TWO_PI * pos_ref[...]
    trig = jnp.concatenate([jnp.cos(angle), jnp.sin(angle)], axis=0)
    for p in range(n):
        pack[p, 0:fpd, :] = ft[p * fpd : (p + 1) * fpd]
        pack[p, fpd : fpd + 6, :] = trig
    pl.semaphore_wait(barrier, n - 1)

    def feat_copy(p, slot):
        return pltpu.make_async_remote_copy(
            src_ref=pack.at[p], dst_ref=fall.at[slot], send_sem=fs.at[p], recv_sem=fr.at[slot],
            device_id=coords(p), device_id_type=MESH)

    def spec_copy(j, slot):
        return pltpu.make_async_remote_copy(
            src_ref=spack_ref.at[j], dst_ref=spall.at[slot], send_sem=ss.at[j], recv_sem=sr.at[slot],
            device_id=coords(ib * nj + j), device_id_type=MESH)

    def halo_copy(side):
        p = me + 1 if side == 0 else me - 1
        return pltpu.make_async_remote_copy(
            src_ref=feat_ref, dst_ref=halo.at[side], send_sem=hs.at[side], recv_sem=hr.at[side],
            device_id=coords(p), device_id_type=MESH)

    def back_copy(p, slot):
        return pltpu.make_async_remote_copy(
            src_ref=lng.at[p], dst_ref=back.at[slot], send_sem=bs.at[p], recv_sem=br.at[slot],
            device_id=coords(p), device_id_type=MESH)

    @pl.when(me + 1 < n)
    def _():
        halo_copy(0).start()

    @pl.when(me > 0)
    def _():
        halo_copy(1).start()

    def send_feat(t, _):
        feat_copy(lax.rem(me + t, n), me).start()
        return 0

    lax.fori_loop(1, n, send_feat, 0)

    def send_spec(t, _):
        spec_copy(lax.rem(mine + t, nj), mine).start()
        return 0

    lax.fori_loop(1, nj, send_spec, 0)
    fall[pl.ds(me, 1)] = pack[pl.ds(me, 1)]
    spall[pl.ds(mine, 1)] = spack_ref[pl.ds(mine, 1)]

    @pl.when(me == 0)
    def _():
        halo[0] = jnp.zeros((rows, width), F32)

    @pl.when(me == n - 1)
    def _():
        halo[1] = jnp.zeros((rows, width), F32)

    own = split(feat_ref[...])
    selft[...] = 0.5 * mm3(own, split(wself_ref[...])).T
    wn = split(wneigh_ref[...])
    span = 3 * BLOCK

    def put_window(at, part):
        hi, lo = split(0.5 * mm3(part, wn).T)
        wt[:, at * BLOCK : (at + 1) * BLOCK] = hi
        wt[:, span + at * BLOCK : span + (at + 1) * BLOCK] = lo

    put_window(1, own)
    radial = wedge_ref.shape[0]
    eh, el = split(0.5 * wedge_ref[...].T)
    wt[:, 2 * span : 2 * span + BLOCK] = jnp.concatenate(
        [eh, eh, el, jnp.zeros((width, BLOCK - 3 * radial), BF16)], axis=1)

    @pl.when(me > 0)
    def _():
        halo_copy(0).wait_recv()

    @pl.when(me + 1 < n)
    def _():
        halo_copy(1).wait_recv()

    put_window(0, split(halo[0]))
    put_window(2, split(halo[1]))

    acc[...] = jnp.zeros((width, rows), F32)
    spacing = REACH / (radial - 1)
    centers = lax.broadcasted_iota(jnp.int32, (radial, rows), 0).astype(F32) * spacing
    row_id = lax.broadcasted_iota(jnp.int32, (span, rows), 0)
    slots = slot_ref.shape[0]
    count = count_ref[...]

    def short_step(t, _):
        parts = []
        for u in range(SLOTS):
            s = t * SLOTS + u
            one = jnp.where(row_id == slot_ref[pl.ds(s, 1), :], 1.0, 0.0).astype(BF16)
            bh, bl = split(jnp.exp(-jnp.square((dist_ref[pl.ds(s, 1), :] - centers) / spacing)))
            parts.append(jnp.concatenate(
                [one, one, bh, bl, bh, jnp.zeros((BLOCK - 3 * radial, rows), BF16)], axis=0))
        pre = dot(wt[...], jnp.concatenate(parts, axis=1))
        total = acc[...]
        for u in range(SLOTS):
            h = pre[:, u * rows : (u + 1) * rows] + selft[...]
            live = count > t * SLOTS + u
            total = total + jnp.where(live, h + h * jnp.tanh(h), 0.0)
        acc[...] = total
        return 0

    lax.fori_loop(0, slots // SLOTS, short_step, 0)
    short = mm3(split((acc[...] * (1.0 / slots)).T), split(wmsg_ref[...]))
    out_ref[...] = feat_ref[...] + short

    def wait_spec(t, _):
        j = lax.rem(mine + t, nj)
        spec_copy(j, j).wait_recv()
        return 0

    lax.fori_loop(1, nj, wait_spec, 0)
    nvec = 4 * HALF * TAB
    gacc[...] = jnp.zeros(gacc.shape, F32)

    def spec_step(j, _):
        sp = spall[j, 0:fpd, :]
        if fp > fpd:
            sp = jnp.concatenate([sp, jnp.zeros((fp - fpd, kloc), F32)], axis=0)
        kx, ky, kz = (spall[j, fpd + i : fpd + i + 1, :] for i in range(3))
        flip = jnp.where(kx < 0, -1.0, 1.0)
        ky, kz = ky * flip, kz * flip
        kind = jnp.where(ky < 0, 2.0, 0.0) + jnp.where(kz < 0, 1.0, 0.0)
        at = kind * (HALF * TAB) + jnp.abs(kx) * TAB + jnp.abs(ky)
        vec_id = lax.broadcasted_iota(jnp.int32, (nvec, kloc), 0).astype(F32)
        pick = jnp.where(vec_id == at, 1.0, 0.0).astype(BF16)
        c = jnp.abs(kz)
        vals = jnp.concatenate([jnp.where(c == i, sp, 0.0) for i in range(TAB)], axis=0)
        hits = jnp.concatenate(
            [jnp.broadcast_to(jnp.where(c == i, 1.0, 0.0), (fp, kloc)) for i in range(TAB)], axis=0)
        vh, vl = split(vals)
        gacc[...] += dot(pick, jnp.concatenate([vh, vl, hits.astype(BF16)], axis=0), 1, 1)
        return 0

    lax.fori_loop(0, nj, spec_step, 0)

    tacc[...] = jnp.zeros(tacc.shape, F32)

    def fwd_step(t, _):
        q = lax.rem(lax.div(me, GROUP) + t, nq)
        for i in range(GROUP):
            p = q * GROUP + i

            @pl.when(p != me)
            def _():
                feat_copy(p, p).wait_recv()

        blocks = [fall[q * GROUP + i] for i in range(GROUP)]
        f = jnp.concatenate([b[0:fpd] for b in blocks], axis=1)
        if fp > fpd:
            f = jnp.concatenate([f, jnp.zeros((fp - fpd, ch), F32)], axis=0)
        c1 = jnp.concatenate([b[fpd : fpd + 3] for b in blocks], axis=1)
        s1 = jnp.concatenate([b[fpd + 3 : fpd + 6] for b in blocks], axis=1)
        cs, sn = [jnp.ones_like(c1), c1], [jnp.zeros_like(c1), s1]
        for a in range(2, HALF):
            cs.append(cs[-1] * c1 - sn[-1] * s1)
            sn.append(sn[-1] * c1 + cs[-2] * s1)
        zero = jnp.zeros((1, ch), F32)
        for a in range(HALF):
            ytab[a : a + 1, :] = cs[a][1:2]
            ytab[TAB + a : TAB + a + 1, :] = sn[a][1:2]
            ztab[q, a : a + 1, :] = cs[a][2:3]
            ztab[q, TAB + a : TAB + a + 1, :] = sn[a][2:3]
        for a in (HALF, TAB + HALF):
            ytab[a : a + 1, :] = zero
            ztab[q, a : a + 1, :] = zero
        yt = ytab[...]
        for a in range(2 * HALF):
            x = cs[a][0:1] if a < HALF else sn[a - HALF][0:1]
            hi, lo = split(x * yt)
            xyh[q, a * 2 * TAB : (a + 1) * 2 * TAB, :] = hi
            xyl[q, a * 2 * TAB : (a + 1) * 2 * TAB, :] = lo
        for c in range(2 * TAB):
            hi, lo = split(ztab[q, c : c + 1, :] * f)
            ah[c * fp : (c + 1) * fp, :] = hi
            al[c * fp : (c + 1) * fp, :] = lo
        tacc[...] += mm3((xyh[q], xyl[q]), (ah[...], al[...]), 1, 1)
        return 0

    lax.fori_loop(0, nq, fwd_step, 0)

    nt = HALF * TAB
    t3 = tacc[...].reshape(2 * HALF, 2 * TAB, 2 * cf)

    def get(x, y, z):
        return t3[x * HALF : (x + 1) * HALF, y * TAB : (y + 1) * TAB, z * cf : (z + 1) * cf].reshape(nt, cf)

    ccc, ccs, csc, css = get(0, 0, 0), get(0, 0, 1), get(0, 1, 0), get(0, 1, 1)
    scc, scs, ssc, sss = get(1, 0, 0), get(1, 0, 1), get(1, 1, 0), get(1, 1, 1)
    pairs, power = [], jnp.zeros((1, cf), F32)
    for v, (b, c) in enumerate(((1, 1), (1, -1), (-1, 1), (-1, -1))):
        cosf = ccc - b * ssc - c * scs - (b * c) * css
        sinf = scc + b * csc + c * ccs - (b * c) * sss
        hits = gacc[v * nt : (v + 1) * nt, 2 * cf : 3 * cf]
        power = power + jnp.sum(hits * (cosf * cosf + sinf * sinf), axis=0, keepdims=True)
        pairs.append((b, c, cosf, sinf))
    for i in range(3):
        power = power + pltpu.roll(power, fp << i, 1)
    kvec = nj * kloc
    scale = lax.rsqrt(power / (2 * kvec) + EPS) * (1.0 / kvec**0.5)
    grid = [jnp.zeros((nt, cf), F32)] * 8
    for v, (b, c, cosf, sinf) in enumerate(pairs):
        g = (gacc[v * nt : (v + 1) * nt, 0:cf] + gacc[v * nt : (v + 1) * nt, cf : 2 * cf]) * scale
        fc, fsn = g * cosf, g * sinf
        signs = (1, c, b, -b * c, 1, -c, -b, -b * c)
        picks = (fc, fsn, fsn, fc, fsn, fc, fc, fsn)
        grid = [old + s * x for old, s, x in zip(grid, signs, picks)]
    g3 = [x.reshape(HALF, TAB, cf) for x in grid]
    plane = [jnp.concatenate([g3[2 * i], g3[2 * i + 1]], axis=2) for i in range(4)]
    half = [jnp.concatenate([plane[2 * i], plane[2 * i + 1]], axis=1) for i in range(2)]
    tt = split(jnp.concatenate(half, axis=0).reshape(2 * HALF * 2 * TAB, 2 * cf).T)

    def inv_step(t, _):
        q = lax.rem(lax.div(me, GROUP) + t, nq)
        field = mm3(tt, (xyh[q], xyl[q]))
        total = jnp.zeros((fp, ch), F32)
        for c in range(2 * TAB):
            if c % TAB < HALF and c != TAB:
                total = total + ztab[q, c : c + 1, :] * field[c * fp : (c + 1) * fp]
        for i in range(GROUP):
            p = q * GROUP + i
            lng[p] = total[0:fpd, i * BLOCK : (i + 1) * BLOCK]

            @pl.when(p != me)
            def _():
                back_copy(p, me).start()

        return 0

    lax.fori_loop(0, nq, inv_step, 0)
    back[pl.ds(me, 1)] = lng[pl.ds(me, 1)]

    def wait_back(t, _):
        p = lax.rem(me + t, n)
        back_copy(p, p).wait_recv()
        return 0

    lax.fori_loop(1, n, wait_back, 0)
    for p in range(n):
        lt[p * fpd : (p + 1) * fpd, :] = back[p]
    total = out_ref[...] + lt[...].T
    normed = total * lax.rsqrt(jnp.mean(total * total, axis=1, keepdims=True) + EPS) * gain_ref[...]
    up = mm3(split(normed), split(wup_ref[...]))
    h = 0.5 * up
    out_ref[...] = total + mm3(split(h + h * jnp.tanh(h)), split(wdown_ref[...]))

    def wait_sent(t, _):
        p = lax.rem(me + t, n)
        feat_copy(p, me).wait_send()
        back_copy(p, me).wait_send()
        return 0

    lax.fori_loop(1, n, wait_sent, 0)

    def wait_spec_sent(t, _):
        spec_copy(lax.rem(mine + t, nj), mine).wait_send()
        return 0

    lax.fori_loop(1, nj, wait_spec_sent, 0)

    @pl.when(me + 1 < n)
    def _():
        halo_copy(0).wait_send()

    @pl.when(me > 0)
    def _():
        halo_copy(1).wait_send()


def local(
    sizes, features, positions, wavevectors, neighbour_slots, neighbour_count, pair_distance,
    w_self, w_neighbour, w_edge, w_message, spec_filter, norm_gain, w_up, w_down,
):
    nb, nw, ng = sizes
    n, nj = nb * nw * ng, nw * ng
    rows, width = features.shape
    kloc = spec_filter.shape[0]
    fpd = width // n
    fp = max(fpd, 16)
    cf = TAB * fp
    ch = GROUP * BLOCK
    nq = n // GROUP
    nxy = 2 * HALF * 2 * TAB
    mine = lax.dynamic_slice_in_dim(spec_filter, lax.axis_index("bead") * (nj * fpd), nj * fpd, 1)
    vectors = jnp.broadcast_to(wavevectors.astype(F32)[None], (nj, 3, kloc))
    spack = jnp.concatenate([mine.T.reshape(nj, fpd, kloc), vectors], axis=1)
    vmem = pl.BlockSpec(memory_space=pltpu.VMEM)
    dma = pltpu.SemaphoreType.DMA
    return pl.pallas_call(
        functools.partial(body, sizes),
        out_shape=jax.ShapeDtypeStruct((rows, width), F32),
        in_specs=[vmem] * 13,
        out_specs=vmem,
        scratch_shapes=[
            pltpu.VMEM((n, fpd + 6, BLOCK), F32),
            pltpu.VMEM((n, fpd + 6, BLOCK), F32),
            pltpu.VMEM((nj, fpd + 3, kloc), F32),
            pltpu.VMEM((2, rows, width), F32),
            pltpu.VMEM((nq, nxy, ch), BF16),
            pltpu.VMEM((nq, nxy, ch), BF16),
            pltpu.VMEM((nq, 2 * TAB, ch), F32),
            pltpu.VMEM((2 * TAB, ch), F32),
            pltpu.VMEM((2 * cf, ch), BF16),
            pltpu.VMEM((2 * cf, ch), BF16),
            pltpu.VMEM((nxy, 2 * cf), F32),
            pltpu.VMEM((n, fpd, BLOCK), F32),
            pltpu.VMEM((n, fpd, BLOCK), F32),
            pltpu.VMEM((width, rows), F32),
            pltpu.VMEM((width, 7 * BLOCK), BF16),
            pltpu.VMEM((width, rows), F32),
            pltpu.VMEM((width, rows), F32),
            pltpu.VMEM((4 * HALF * TAB, 3 * cf), F32),
            dma((n,)), dma((n,)), dma((nj,)), dma((nj,)), dma((2,)), dma((2,)), dma((n,)), dma((n,)),
        ],
        compiler_params=pltpu.CompilerParams(
            collective_id=0, has_side_effects=True, vmem_limit_bytes=60 * 1024 * 1024),
        cost_estimate=pl.CostEstimate(flops=10**10, bytes_accessed=10**7, transcendentals=10**7),
    )(
        features, positions, spack, neighbour_slots, neighbour_count[None], pair_distance,
        w_self, w_neighbour, w_edge, w_message, norm_gain[None], w_up, w_down,
    )


def solution(mesh):
    sizes = tuple(mesh.shape[a] for a in ("bead", "wave", "grp"))
    every = ("bead", "wave", "grp")
    placed = (
        P(every, None), P(None, every), P(None, ("wave", "grp")), P(None, every), P(every), P(None, every),
        P(), P(), P(), P(), P(("wave", "grp"), None), P(), P(), P(),
    )
    return jax.shard_map(
        functools.partial(local, sizes), mesh=mesh, in_specs=placed, out_specs=P(every, None), check_vma=False)
```

```python
import functools

import jax
import jax.numpy as jnp
from jax import lax
from jax.experimental import pallas as pl
from jax.experimental.pallas import tpu as pltpu
from jax.sharding import PartitionSpec as P

MESH = pl.DeviceIdType.MESH
F32, BF16 = jnp.float32, jnp.bfloat16
BLOCK = 128
TOP = 6
HALF = TOP + 1
TAB = 8
REACH = 2.5
EPS = 1e-05
TWO_PI = 6.283185307179586
GROUP = 4
SLOTS = 4


def split(x):
    hi = x.astype(BF16)
    return hi, (x - hi.astype(F32)).astype(BF16)


def dot(a, b, ca=1, cb=0):
    return lax.dot_general(a, b, (((ca,), (cb,)), ((), ())), preferred_element_type=F32)


def mm3(a, b, ca=1, cb=0):
    return dot(a[0], b[0], ca, cb) + (dot(a[0], b[1], ca, cb) + dot(a[1], b[0], ca, cb))


def body(
    sizes,
    feat_ref, pos_ref, wave_ref, slot_ref, count_ref, dist_ref, wedge_ref, gain_ref,
    spec_hbm, wself_hbm, wneigh_hbm, wmsg_hbm, wup_hbm, wdown_hbm,
    out_ref,
    pack, fall, spack, spall, tall, wall, halo, xyh, xyl, ztab, ytab, ah, al, tacc, lng, back, lt,
    wt, selft, acc, gacc, spec, weights,
    fs, fr, ss, sr, hs, hr, bs, br, t1s, t1r, t2s, t2r, w1s, w1r, w2s, w2r, ls,
):
    nb, nw, ng = sizes
    n, nj = nb * nw * ng, nw * ng
    rows, width = feat_ref.shape
    fpd = width // n
    fp = max(fpd, 16)
    cf = TAB * fp
    ch = GROUP * BLOCK
    nq = n // GROUP
    kloc = spec_hbm.shape[0]
    cols = nj * fpd
    nr = nb * ng
    ib, iw, ig = lax.axis_index("bead"), lax.axis_index("wave"), lax.axis_index("grp")
    mine = iw * ng + ig
    me = ib * nj + mine

    def coords(p):
        return (lax.div(p, nj), lax.rem(lax.div(p, ng), nw), lax.rem(p, ng))

    at = ib * cols
    source = spec_hbm if cols % 128 else spec_hbm.at[:, pl.ds(pl.multiple_of(at, 128), cols)]
    fetch = [pltpu.make_async_copy(source, spec, ls.at[0])]
    for i, w in enumerate((wself_hbm, wneigh_hbm, wmsg_hbm, wup_hbm, wdown_hbm)):
        fetch.append(pltpu.make_async_copy(w, weights.at[i], ls.at[i + 1]))
    for copy in fetch:
        copy.start()

    barrier = pltpu.get_barrier_semaphore()

    def greet(t, _):
        pl.semaphore_signal(barrier, inc=1, device_id=coords(lax.rem(me + t, n)), device_id_type=MESH)
        return 0

    lax.fori_loop(1, n, greet, 0)

    ft = feat_ref[...].T
    angle = TWO_PI * pos_ref[...]
    trig = jnp.concatenate([jnp.cos(angle), jnp.sin(angle), jnp.zeros((2, rows), F32)], axis=0)
    tall[ib, ig, iw] = trig
    wall[ig, iw] = wave_ref[...]
    for p in range(n):
        pack[p] = ft[p * fpd : (p + 1) * fpd]
    pl.semaphore_wait(barrier, n - 1)

    def along_copies(w, slot):
        return [pltpu.make_async_remote_copy(
            src_ref=buf.at[ig, iw] if buf is wall else buf.at[ib, ig, iw],
            dst_ref=buf.at[ig, slot] if buf is wall else buf.at[ib, ig, slot],
            send_sem=send.at[w], recv_sem=recv.at[slot],
            device_id=(ib, w, ig), device_id_type=MESH) for buf, send, recv in ((tall, t1s, t1r), (wall, w1s, w1r))]

    def plane_copy(r, slot):
        b, g = lax.div(slot, ng), lax.rem(slot, ng)
        return pltpu.make_async_remote_copy(
            src_ref=tall.at[ib, ig], dst_ref=tall.at[b, g], send_sem=t2s.at[r], recv_sem=t2r.at[slot],
            device_id=(lax.div(r, ng), iw, lax.rem(r, ng)), device_id_type=MESH)

    def core_copy(g, slot):
        return pltpu.make_async_remote_copy(
            src_ref=wall.at[ig], dst_ref=wall.at[slot], send_sem=w2s.at[g], recv_sem=w2r.at[slot],
            device_id=(ib, iw, g), device_id_type=MESH)

    def feat_copy(p, slot):
        return pltpu.make_async_remote_copy(
            src_ref=pack.at[p], dst_ref=fall.at[slot], send_sem=fs.at[p], recv_sem=fr.at[slot],
            device_id=coords(p), device_id_type=MESH)

    def spec_copy(j, slot):
        return pltpu.make_async_remote_copy(
            src_ref=spack.at[j], dst_ref=spall.at[slot], send_sem=ss.at[j], recv_sem=sr.at[slot],
            device_id=coords(ib * nj + j), device_id_type=MESH)

    def halo_copy(side):
        p = me + 1 if side == 0 else me - 1
        return pltpu.make_async_remote_copy(
            src_ref=feat_ref, dst_ref=halo.at[side], send_sem=hs.at[side], recv_sem=hr.at[side],
            device_id=coords(p), device_id_type=MESH)

    def back_copy(p, slot):
        return pltpu.make_async_remote_copy(
            src_ref=lng.at[p], dst_ref=back.at[slot], send_sem=bs.at[p], recv_sem=br.at[slot],
            device_id=coords(p), device_id_type=MESH)

    for k in range(1, nw):
        for copy in along_copies(lax.rem(iw + k, nw), iw):
            copy.start()
    here = ib * ng + ig
    far = sorted(range(nw), key=lambda k: -min(k, nw - k))
    for k in far:
        w = lax.rem(iw + k, nw)

        def send_feat(t, _):
            r = lax.rem(here + t, nr)
            feat_copy((lax.div(r, ng) * nw + w) * ng + lax.rem(r, ng), me).start()
            return 0

        lax.fori_loop(0 if k else 1, nr, send_feat, 0)

    fetch[0].wait()
    st = spec[...].T
    for j in range(nj):
        spack[j] = st[j * fpd : (j + 1) * fpd]
    for k in range(1, nw):
        for copy in along_copies(iw, lax.rem(iw + k, nw)):
            copy.wait_recv()

    def send_plane(t, _):
        plane_copy(lax.rem(here + t, nr), here).start()
        return 0

    lax.fori_loop(1, nr, send_plane, 0)
    for k in range(1, ng):
        core_copy(lax.rem(ig + k, ng), ig).start()

    def send_spec(t, _):
        j = lax.rem(mine + nj // 2 + t, nj)

        @pl.when(j != mine)
        def _():
            spec_copy(j, mine).start()

        return 0

    lax.fori_loop(0, nj, send_spec, 0)
    fall[pl.ds(me, 1)] = pack[pl.ds(me, 1)]
    spall[pl.ds(mine, 1)] = spack[pl.ds(mine, 1)]

    @pl.when(me == 0)
    def _():
        halo[0] = jnp.zeros((rows, width), F32)

    @pl.when(me == n - 1)
    def _():
        halo[1] = jnp.zeros((rows, width), F32)

    fetch[1].wait()
    own = split(feat_ref[...])
    selft[...] = 0.5 * mm3(own, split(weights[0])).T
    fetch[2].wait()
    wn = split(weights[1])
    span = 3 * BLOCK

    def put_window(at, part):
        hi, lo = split(0.5 * mm3(part, wn).T)
        wt[:, at * BLOCK : (at + 1) * BLOCK] = hi
        wt[:, span + at * BLOCK : span + (at + 1) * BLOCK] = lo

    put_window(1, own)
    radial = wedge_ref.shape[0]
    eh, el = split(0.5 * wedge_ref[...].T)
    wt[:, 2 * span : 2 * span + BLOCK] = jnp.concatenate(
        [eh, eh, el, jnp.zeros((width, BLOCK - 3 * radial), BF16)], axis=1)

    for i in range(3, 6):
        fetch[i].wait()

    tacc[...] = jnp.zeros(tacc.shape, F32)

    def wait_plane(t, _):
        r = lax.rem(here + t, nr)
        plane_copy(r, r).wait_recv()
        return 0

    lax.fori_loop(1, nr, wait_plane, 0)
    for k in range(1, ng):
        core_copy(ig, lax.rem(ig + k, ng)).wait_recv()
    per = nq // nb
    first = lax.div(mine, GROUP)

    def chunk(t):
        return lax.rem(ib + t, nb) * per + lax.rem(first + lax.div(t, nb), per)

    def fwd_step(t, _):
        q = chunk(t)
        for i in range(GROUP):
            p = q * GROUP + i

            @pl.when(p != me)
            def _():
                feat_copy(p, p).wait_recv()

        blocks = [fall[q * GROUP + i] for i in range(GROUP)]
        f = jnp.concatenate(blocks, axis=1)
        if fp > fpd:
            f = jnp.concatenate([f, jnp.zeros((fp - fpd, ch), F32)], axis=0)
        places = [(lax.div(p, nj), lax.rem(p, ng), lax.rem(lax.div(p, ng), nw)) for p in [q * GROUP + i for i in range(GROUP)]]
        trigs = jnp.concatenate([tall[b, g, w] for b, g, w in places], axis=1)
        c1, s1 = trigs[0:3], trigs[3:6]
        cs, sn = [jnp.ones_like(c1), c1], [jnp.zeros_like(c1), s1]
        for a in range(2, HALF):
            cs.append(cs[-1] * c1 - sn[-1] * s1)
            sn.append(sn[-1] * c1 + cs[-2] * s1)
        zero = jnp.zeros((1, ch), F32)
        for a in range(HALF):
            ytab[a : a + 1, :] = cs[a][1:2]
            ytab[TAB + a : TAB + a + 1, :] = sn[a][1:2]
            ztab[q, a : a + 1, :] = cs[a][2:3]
            ztab[q, TAB + a : TAB + a + 1, :] = sn[a][2:3]
        for a in (HALF, TAB + HALF):
            ytab[a : a + 1, :] = zero
            ztab[q, a : a + 1, :] = zero
        yt = ytab[...]
        for a in range(2 * HALF):
            x = cs[a][0:1] if a < HALF else sn[a - HALF][0:1]
            hi, lo = split(x * yt)
            xyh[q, a * 2 * TAB : (a + 1) * 2 * TAB, :] = hi
            xyl[q, a * 2 * TAB : (a + 1) * 2 * TAB, :] = lo
        for c in range(2 * TAB):
            hi, lo = split(ztab[q, c : c + 1, :] * f)
            ah[c * fp : (c + 1) * fp, :] = hi
            al[c * fp : (c + 1) * fp, :] = lo
        tacc[...] += mm3((xyh[q], xyl[q]), (ah[...], al[...]), 1, 1)
        return 0

    lax.fori_loop(0, nq, fwd_step, 0)

    @pl.when(me + 1 < n)
    def _():
        halo_copy(0).start()

    @pl.when(me > 0)
    def _():
        halo_copy(1).start()

    def wait_spec(t, _):
        j = lax.rem(mine + t, nj)
        spec_copy(j, j).wait_recv()
        return 0

    lax.fori_loop(1, nj, wait_spec, 0)
    nvec = 4 * HALF * TAB
    gacc[...] = jnp.zeros(gacc.shape, F32)

    def spec_step(j, _):
        sp = spall[j]
        if fp > fpd:
            sp = jnp.concatenate([sp, jnp.zeros((fp - fpd, kloc), F32)], axis=0)
        vec = wall[lax.rem(j, ng), lax.div(j, ng)].astype(F32)
        kx, ky, kz = (vec[i : i + 1] for i in range(3))
        flip = jnp.where(kx < 0, -1.0, 1.0)
        ky, kz = ky * flip, kz * flip
        kind = jnp.where(ky < 0, 2.0, 0.0) + jnp.where(kz < 0, 1.0, 0.0)
        at = kind * (HALF * TAB) + jnp.abs(kx) * TAB + jnp.abs(ky)
        vec_id = lax.broadcasted_iota(jnp.int32, (nvec, kloc), 0).astype(F32)
        pick = jnp.where(vec_id == at, 1.0, 0.0).astype(BF16)
        c = jnp.abs(kz)
        vals = jnp.concatenate([jnp.where(c == i, sp, 0.0) for i in range(TAB)], axis=0)
        hits = jnp.concatenate(
            [jnp.broadcast_to(jnp.where(c == i, 1.0, 0.0), (fp, kloc)) for i in range(TAB)], axis=0)
        vh, vl = split(vals)
        gacc[...] += dot(pick, jnp.concatenate([vh, vl, hits.astype(BF16)], axis=0), 1, 1)
        return 0

    lax.fori_loop(0, nj, spec_step, 0)

    nt = HALF * TAB
    t3 = tacc[...].reshape(2 * HALF, 2 * TAB, 2 * cf)

    def get(x, y, z):
        return t3[x * HALF : (x + 1) * HALF, y * TAB : (y + 1) * TAB, z * cf : (z + 1) * cf].reshape(nt, cf)

    ccc, ccs, csc, css = get(0, 0, 0), get(0, 0, 1), get(0, 1, 0), get(0, 1, 1)
    scc, scs, ssc, sss = get(1, 0, 0), get(1, 0, 1), get(1, 1, 0), get(1, 1, 1)
    pairs, power = [], jnp.zeros((1, cf), F32)
    for v, (b, c) in enumerate(((1, 1), (1, -1), (-1, 1), (-1, -1))):
        cosf = ccc - b * ssc - c * scs - (b * c) * css
        sinf = scc + b * csc + c * ccs - (b * c) * sss
        hits = gacc[v * nt : (v + 1) * nt, 2 * cf : 3 * cf]
        power = power + jnp.sum(hits * (cosf * cosf + sinf * sinf), axis=0, keepdims=True)
        pairs.append((b, c, cosf, sinf))
    for i in range(3):
        power = power + pltpu.roll(power, fp << i, 1)
    kvec = nj * kloc
    scale = lax.rsqrt(power / (2 * kvec) + EPS) * (1.0 / kvec**0.5)
    grid = [jnp.zeros((nt, cf), F32)] * 8
    for v, (b, c, cosf, sinf) in enumerate(pairs):
        g = (gacc[v * nt : (v + 1) * nt, 0:cf] + gacc[v * nt : (v + 1) * nt, cf : 2 * cf]) * scale
        fc, fsn = g * cosf, g * sinf
        signs = (1, c, b, -b * c, 1, -c, -b, -b * c)
        picks = (fc, fsn, fsn, fc, fsn, fc, fc, fsn)
        grid = [old + s * x for old, s, x in zip(grid, signs, picks)]
    g3 = [x.reshape(HALF, TAB, cf) for x in grid]
    plane = [jnp.concatenate([g3[2 * i], g3[2 * i + 1]], axis=2) for i in range(4)]
    half = [jnp.concatenate([plane[2 * i], plane[2 * i + 1]], axis=1) for i in range(2)]
    tt = split(jnp.concatenate(half, axis=0).reshape(2 * HALF * 2 * TAB, 2 * cf).T)

    def inv_step(t, _):
        q = chunk(nq - 1 - t)
        field = mm3(tt, (xyh[q], xyl[q]))
        total = jnp.zeros((fp, ch), F32)
        for c in range(2 * TAB):
            if c % TAB < HALF and c != TAB:
                total = total + ztab[q, c : c + 1, :] * field[c * fp : (c + 1) * fp]
        for i in range(GROUP):
            p = q * GROUP + i
            lng[p] = total[0:fpd, i * BLOCK : (i + 1) * BLOCK]

            @pl.when(p != me)
            def _():
                back_copy(p, me).start()

        return 0

    lax.fori_loop(0, nq, inv_step, 0)
    back[pl.ds(me, 1)] = lng[pl.ds(me, 1)]

    @pl.when(me > 0)
    def _():
        halo_copy(0).wait_recv()

    @pl.when(me + 1 < n)
    def _():
        halo_copy(1).wait_recv()

    put_window(0, split(halo[0]))
    put_window(2, split(halo[1]))

    acc[...] = jnp.zeros((width, rows), F32)
    spacing = REACH / (radial - 1)
    centers = lax.broadcasted_iota(jnp.int32, (radial, rows), 0).astype(F32) * spacing
    row_id = lax.broadcasted_iota(jnp.int32, (span, rows), 0)
    slots = slot_ref.shape[0]
    count = count_ref[...]

    def short_step(t, _):
        parts = []
        for u in range(SLOTS):
            s = t * SLOTS + u
            one = jnp.where(row_id == slot_ref[pl.ds(s, 1), :], 1.0, 0.0).astype(BF16)
            bh, bl = split(jnp.exp(-jnp.square((dist_ref[pl.ds(s, 1), :] - centers) / spacing)))
            parts.append(jnp.concatenate(
                [one, one, bh, bl, bh, jnp.zeros((BLOCK - 3 * radial, rows), BF16)], axis=0))
        pre = dot(wt[...], jnp.concatenate(parts, axis=1))
        total = acc[...]
        for u in range(SLOTS):
            h = pre[:, u * rows : (u + 1) * rows] + selft[...]
            live = count > t * SLOTS + u
            total = total + jnp.where(live, h + h * jnp.tanh(h), 0.0)
        acc[...] = total
        return 0

    lax.fori_loop(0, slots // SLOTS, short_step, 0)
    short = mm3(split((acc[...] * (1.0 / slots)).T), split(weights[2]))
    out_ref[...] = feat_ref[...] + short


    def wait_back(t, _):
        p = lax.rem(me + t, n)
        back_copy(p, p).wait_recv()
        return 0

    lax.fori_loop(1, n, wait_back, 0)
    for p in range(n):
        lt[p * fpd : (p + 1) * fpd, :] = back[p]
    total = out_ref[...] + lt[...].T
    normed = total * lax.rsqrt(jnp.mean(total * total, axis=1, keepdims=True) + EPS) * gain_ref[...]
    up = mm3(split(normed), split(weights[3]))
    h = 0.5 * up
    out_ref[...] = total + mm3(split(h + h * jnp.tanh(h)), split(weights[4]))

    def wait_sent(t, _):
        p = lax.rem(me + t, n)
        feat_copy(p, me).wait_send()
        back_copy(p, me).wait_send()
        return 0

    lax.fori_loop(1, n, wait_sent, 0)

    for k in range(1, nw):
        for copy in along_copies(lax.rem(iw + k, nw), iw):
            copy.wait_send()

    def wait_plane_sent(t, _):
        plane_copy(lax.rem(here + t, nr), here).wait_send()
        return 0

    lax.fori_loop(1, nr, wait_plane_sent, 0)
    for k in range(1, ng):
        core_copy(lax.rem(ig + k, ng), ig).wait_send()

    def wait_spec_sent(t, _):
        spec_copy(lax.rem(mine + t, nj), mine).wait_send()
        return 0

    lax.fori_loop(1, nj, wait_spec_sent, 0)

    @pl.when(me + 1 < n)
    def _():
        halo_copy(0).wait_send()

    @pl.when(me > 0)
    def _():
        halo_copy(1).wait_send()


def local(
    sizes, features, positions, wavevectors, neighbour_slots, neighbour_count, pair_distance,
    w_self, w_neighbour, w_edge, w_message, spec_filter, norm_gain, w_up, w_down,
):
    nb, nw, ng = sizes
    n, nj = nb * nw * ng, nw * ng
    rows, width = features.shape
    kloc = spec_filter.shape[0]
    fpd = width // n
    fp = max(fpd, 16)
    cf = TAB * fp
    ch = GROUP * BLOCK
    nq = n // GROUP
    nxy = 2 * HALF * 2 * TAB
    cols = nj * fpd
    if cols % 128:
        spec_filter = lax.dynamic_slice_in_dim(spec_filter, lax.axis_index("bead") * cols, cols, 1)
    vmem = pl.BlockSpec(memory_space=pltpu.VMEM)
    dma = pltpu.SemaphoreType.DMA
    return pl.pallas_call(
        functools.partial(body, sizes),
        out_shape=jax.ShapeDtypeStruct((rows, width), F32),
        in_specs=[vmem] * 8 + [pl.BlockSpec(memory_space=pl.ANY)] * 6,
        out_specs=vmem,
        scratch_shapes=[
            pltpu.VMEM((n, fpd, BLOCK), F32),
            pltpu.VMEM((n, fpd, BLOCK), F32),
            pltpu.VMEM((nj, fpd, kloc), F32),
            pltpu.VMEM((nj, fpd, kloc), F32),
            pltpu.VMEM((nb, ng, nw, 8, BLOCK), F32),
            pltpu.VMEM((ng, nw, 3, kloc), jnp.int32),
            pltpu.VMEM((2, rows, width), F32),
            pltpu.VMEM((nq, nxy, ch), BF16),
            pltpu.VMEM((nq, nxy, ch), BF16),
            pltpu.VMEM((nq, 2 * TAB, ch), F32),
            pltpu.VMEM((2 * TAB, ch), F32),
            pltpu.VMEM((2 * cf, ch), BF16),
            pltpu.VMEM((2 * cf, ch), BF16),
            pltpu.VMEM((nxy, 2 * cf), F32),
            pltpu.VMEM((n, fpd, BLOCK), F32),
            pltpu.VMEM((n, fpd, BLOCK), F32),
            pltpu.VMEM((width, rows), F32),
            pltpu.VMEM((width, 7 * BLOCK), BF16),
            pltpu.VMEM((width, rows), F32),
            pltpu.VMEM((width, rows), F32),
            pltpu.VMEM((4 * HALF * TAB, 3 * cf), F32),
            pltpu.VMEM((kloc, cols), F32),
            pltpu.VMEM((5, width, width), F32),
            dma((n,)), dma((n,)), dma((nj,)), dma((nj,)), dma((2,)), dma((2,)), dma((n,)), dma((n,)),
            dma((nw,)), dma((nw,)), dma((nb * ng,)), dma((nb * ng,)), dma((nw,)), dma((nw,)), dma((ng,)), dma((ng,)), dma((6,)),
        ],
        compiler_params=pltpu.CompilerParams(
            collective_id=0, has_side_effects=True, vmem_limit_bytes=60 * 1024 * 1024),
        cost_estimate=pl.CostEstimate(flops=10**10, bytes_accessed=10**7, transcendentals=10**7),
    )(
        features, positions, wavevectors, neighbour_slots, neighbour_count[None], pair_distance,
        w_edge, norm_gain[None], spec_filter, w_self, w_neighbour, w_message, w_up, w_down,
    )


def solution(mesh):
    sizes = tuple(mesh.shape[a] for a in ("bead", "wave", "grp"))
    every = ("bead", "wave", "grp")
    placed = (
        P(every, None), P(None, every), P(None, ("wave", "grp")), P(None, every), P(every), P(None, every),
        P(), P(), P(), P(), P(("wave", "grp"), None), P(), P(), P(),
    )
    return jax.shard_map(
        functools.partial(local, sizes), mesh=mesh, in_specs=placed, out_specs=P(every, None), check_vma=False)
```

```python
import functools

import jax
import jax.numpy as jnp
from jax import lax
from jax.experimental import pallas as pl
from jax.experimental.pallas import tpu as pltpu
from jax.sharding import PartitionSpec as P

MESH = pl.DeviceIdType.MESH
F32, BF16 = jnp.float32, jnp.bfloat16
BLOCK = 128
TOP = 6
HALF = TOP + 1
TAB = 8
REACH = 2.5
EPS = 1e-05
TWO_PI = 6.283185307179586
GROUP = 4
SLOTS = 4


def split(x):
    hi = x.astype(BF16)
    return hi, (x - hi.astype(F32)).astype(BF16)


def dot(a, b, ca=1, cb=0):
    return lax.dot_general(a, b, (((ca,), (cb,)), ((), ())), preferred_element_type=F32)


def mm3(a, b, ca=1, cb=0):
    return dot(a[0], b[0], ca, cb) + (dot(a[0], b[1], ca, cb) + dot(a[1], b[0], ca, cb))


def body(
    sizes,
    feat_ref, pos_ref, wave_ref, slot_ref, count_ref, dist_ref, wedge_ref, gain_ref,
    spec_hbm, wself_hbm, wneigh_hbm, wmsg_hbm, wup_hbm, wdown_hbm,
    out_ref,
    pack, fall, spack, spall, tall, wall, halo, xyh, xyl, ztab, ytab, ah, al, tacc, lng, back, lt,
    wt, selft, acc, gacc, spec, weights, wide,
    fs, fr, ss, sr, hs, hr, bs, br, t1s, t1r, t2s, t2r, w1s, w1r, w2s, w2r, ls,
):
    nb, nw, ng = sizes
    n, nj = nb * nw * ng, nw * ng
    rows, width = feat_ref.shape
    fpd = width // n
    fp = max(fpd, 16)
    cf = TAB * fp
    ch = GROUP * BLOCK
    nq = n // GROUP
    kloc = spec_hbm.shape[0]
    cols = nj * fpd
    nr = nb * ng
    ib, iw, ig = lax.axis_index("bead"), lax.axis_index("wave"), lax.axis_index("grp")
    mine = iw * ng + ig
    me = ib * nj + mine

    def coords(p):
        return (lax.div(p, nj), lax.rem(lax.div(p, ng), nw), lax.rem(p, ng))

    at = ib * cols
    source = spec_hbm if cols % 128 else spec_hbm.at[:, pl.ds(pl.multiple_of(at, 128), cols)]
    fetch = [pltpu.make_async_copy(source, spec, ls.at[0])]
    for i, w in enumerate((wself_hbm, wneigh_hbm, wmsg_hbm, wup_hbm, wdown_hbm)):
        fetch.append(pltpu.make_async_copy(w, weights.at[i], ls.at[i + 1]))
    for copy in fetch:
        copy.start()

    barrier = pltpu.get_barrier_semaphore()

    def greet(t, _):
        pl.semaphore_signal(barrier, inc=1, device_id=coords(lax.rem(me + t, n)), device_id_type=MESH)
        return 0

    lax.fori_loop(1, n, greet, 0)

    ft = feat_ref[...].T
    angle = TWO_PI * pos_ref[...]
    trig = jnp.concatenate([jnp.cos(angle), jnp.sin(angle), jnp.zeros((2, rows), F32)], axis=0)
    tall[ib, ig, iw] = trig
    wall[ig, iw] = wave_ref[...]
    for p in range(n):
        pack[p] = ft[p * fpd : (p + 1) * fpd]
    pl.semaphore_wait(barrier, n - 1)

    def along_copies(w, slot):
        return [pltpu.make_async_remote_copy(
            src_ref=buf.at[ig, iw] if buf is wall else buf.at[ib, ig, iw],
            dst_ref=buf.at[ig, slot] if buf is wall else buf.at[ib, ig, slot],
            send_sem=send.at[w], recv_sem=recv.at[slot],
            device_id=(ib, w, ig), device_id_type=MESH) for buf, send, recv in ((tall, t1s, t1r), (wall, w1s, w1r))]

    def plane_copy(r, slot):
        b, g = lax.div(slot, ng), lax.rem(slot, ng)
        return pltpu.make_async_remote_copy(
            src_ref=tall.at[ib, ig], dst_ref=tall.at[b, g], send_sem=t2s.at[r], recv_sem=t2r.at[slot],
            device_id=(lax.div(r, ng), iw, lax.rem(r, ng)), device_id_type=MESH)

    def core_copy(g, slot):
        return pltpu.make_async_remote_copy(
            src_ref=wall.at[ig], dst_ref=wall.at[slot], send_sem=w2s.at[g], recv_sem=w2r.at[slot],
            device_id=(ib, iw, g), device_id_type=MESH)

    def feat_copy(p, slot):
        return pltpu.make_async_remote_copy(
            src_ref=pack.at[p], dst_ref=fall.at[slot], send_sem=fs.at[p], recv_sem=fr.at[slot],
            device_id=coords(p), device_id_type=MESH)

    def spec_copy(j, slot):
        return pltpu.make_async_remote_copy(
            src_ref=spack.at[j], dst_ref=spall.at[slot], send_sem=ss.at[j], recv_sem=sr.at[slot],
            device_id=coords(ib * nj + j), device_id_type=MESH)

    def halo_copy(side):
        p = me + 1 if side == 0 else me - 1
        return pltpu.make_async_remote_copy(
            src_ref=feat_ref, dst_ref=halo.at[side], send_sem=hs.at[side], recv_sem=hr.at[side],
            device_id=coords(p), device_id_type=MESH)

    def back_copy(p, slot):
        return pltpu.make_async_remote_copy(
            src_ref=lng.at[p], dst_ref=back.at[slot], send_sem=bs.at[p], recv_sem=br.at[slot],
            device_id=coords(p), device_id_type=MESH)

    for k in range(1, nw):
        for copy in along_copies(lax.rem(iw + k, nw), iw):
            copy.start()
    here = ib * ng + ig
    far = sorted(range(nw), key=lambda k: -min(k, nw - k))
    for k in far:
        w = lax.rem(iw + k, nw)

        def send_feat(t, _):
            r = lax.rem(here + t, nr)
            feat_copy((lax.div(r, ng) * nw + w) * ng + lax.rem(r, ng), me).start()
            return 0

        lax.fori_loop(0 if k else 1, nr, send_feat, 0)

    fetch[0].wait()
    st = spec[...].T
    for j in range(nj):
        spack[j] = st[j * fpd : (j + 1) * fpd]
    for k in range(1, nw):
        for copy in along_copies(iw, lax.rem(iw + k, nw)):
            copy.wait_recv()

    def send_plane(t, _):
        plane_copy(lax.rem(here + t, nr), here).start()
        return 0

    lax.fori_loop(1, nr, send_plane, 0)
    for k in range(1, ng):
        core_copy(lax.rem(ig + k, ng), ig).start()

    def send_spec(t, _):
        j = lax.rem(mine + nj // 2 + t, nj)

        @pl.when(j != mine)
        def _():
            spec_copy(j, mine).start()

        return 0

    lax.fori_loop(0, nj, send_spec, 0)
    fall[pl.ds(me, 1)] = pack[pl.ds(me, 1)]
    spall[pl.ds(mine, 1)] = spack[pl.ds(mine, 1)]

    @pl.when(me == 0)
    def _():
        halo[0] = jnp.zeros((rows, width), F32)

    @pl.when(me == n - 1)
    def _():
        halo[1] = jnp.zeros((rows, width), F32)

    fetch[1].wait()
    own = split(feat_ref[...])
    selft[...] = 0.5 * mm3(own, split(weights[0])).T
    fetch[2].wait()
    wn = split(weights[1])
    span = 3 * BLOCK

    def put_window(at, part):
        wt[:, at * BLOCK : (at + 1) * BLOCK] = (0.5 * mm3(part, wn)).T.astype(BF16)

    put_window(1, own)
    radial = wedge_ref.shape[0]
    eh, el = split(0.5 * wedge_ref[...].T)
    wt[:, span : span + BLOCK] = jnp.concatenate(
        [eh, eh, el, jnp.zeros((width, BLOCK - 3 * radial), BF16)], axis=1)

    for i in range(3):
        fetch[i + 3].wait()
        wide[i, 0], wide[i, 1] = split(weights[i + 2])

    tacc[...] = jnp.zeros(tacc.shape, F32)

    def wait_plane(t, _):
        r = lax.rem(here + t, nr)
        plane_copy(r, r).wait_recv()
        return 0

    lax.fori_loop(1, nr, wait_plane, 0)
    for k in range(1, ng):
        core_copy(ig, lax.rem(ig + k, ng)).wait_recv()
    per = nq // nb
    first = lax.div(mine, GROUP)

    def chunk(t):
        return lax.rem(ib + t, nb) * per + lax.rem(first + lax.div(t, nb), per)

    def fwd_step(t, _):
        q = chunk(t)

        @pl.when((t == nq // 2) & (me + 1 < n))
        def _():
            halo_copy(0).start()

        @pl.when((t == nq // 2) & (me > 0))
        def _():
            halo_copy(1).start()

        for i in range(GROUP):
            p = q * GROUP + i

            @pl.when(p != me)
            def _():
                feat_copy(p, p).wait_recv()

        blocks = [fall[q * GROUP + i] for i in range(GROUP)]
        f = jnp.concatenate(blocks, axis=1)
        if fp > fpd:
            f = jnp.concatenate([f, jnp.zeros((fp - fpd, ch), F32)], axis=0)
        places = [(lax.div(p, nj), lax.rem(p, ng), lax.rem(lax.div(p, ng), nw)) for p in [q * GROUP + i for i in range(GROUP)]]
        trigs = jnp.concatenate([tall[b, g, w] for b, g, w in places], axis=1)
        c1, s1 = trigs[0:3], trigs[3:6]
        cs, sn = [jnp.ones_like(c1), c1], [jnp.zeros_like(c1), s1]
        for a in range(2, HALF):
            cs.append(cs[-1] * c1 - sn[-1] * s1)
            sn.append(sn[-1] * c1 + cs[-2] * s1)
        zero = jnp.zeros((1, ch), F32)
        for a in range(HALF):
            ytab[a : a + 1, :] = cs[a][1:2]
            ytab[TAB + a : TAB + a + 1, :] = sn[a][1:2]
            ztab[q, a : a + 1, :] = cs[a][2:3]
            ztab[q, TAB + a : TAB + a + 1, :] = sn[a][2:3]
        for a in (HALF, TAB + HALF):
            ytab[a : a + 1, :] = zero
            ztab[q, a : a + 1, :] = zero
        yt = ytab[...]
        for a in range(2 * HALF):
            x = cs[a][0:1] if a < HALF else sn[a - HALF][0:1]
            hi, lo = split(x * yt)
            xyh[q, a * 2 * TAB : (a + 1) * 2 * TAB, :] = hi
            xyl[q, a * 2 * TAB : (a + 1) * 2 * TAB, :] = lo
        for c in range(2 * TAB):
            hi, lo = split(ztab[q, c : c + 1, :] * f)
            ah[c * fp : (c + 1) * fp, :] = hi
            al[c * fp : (c + 1) * fp, :] = lo
        tacc[...] += mm3((xyh[q], xyl[q]), (ah[...], al[...]), 1, 1)
        return 0

    lax.fori_loop(0, nq, fwd_step, 0)

    def wait_spec(t, _):
        j = lax.rem(mine + t, nj)
        spec_copy(j, j).wait_recv()
        return 0

    lax.fori_loop(1, nj, wait_spec, 0)
    nvec = 4 * HALF * TAB
    gacc[...] = jnp.zeros(gacc.shape, F32)

    def spec_step(j, _):
        sp = spall[j]
        if fp > fpd:
            sp = jnp.concatenate([sp, jnp.zeros((fp - fpd, kloc), F32)], axis=0)
        vec = wall[lax.rem(j, ng), lax.div(j, ng)].astype(F32)
        kx, ky, kz = (vec[i : i + 1] for i in range(3))
        flip = jnp.where(kx < 0, -1.0, 1.0)
        ky, kz = ky * flip, kz * flip
        kind = jnp.where(ky < 0, 2.0, 0.0) + jnp.where(kz < 0, 1.0, 0.0)
        at = kind * (HALF * TAB) + jnp.abs(kx) * TAB + jnp.abs(ky)
        vec_id = lax.broadcasted_iota(jnp.int32, (nvec, kloc), 0).astype(F32)
        pick = jnp.where(vec_id == at, 1.0, 0.0).astype(BF16)
        c = jnp.abs(kz)
        vals = jnp.concatenate([jnp.where(c == i, sp, 0.0) for i in range(TAB)], axis=0)
        hits = jnp.concatenate(
            [jnp.broadcast_to(jnp.where(c == i, 1.0, 0.0), (fp, kloc)) for i in range(TAB)], axis=0)
        vh, vl = split(vals)
        gacc[...] += dot(pick, jnp.concatenate([vh, vl, hits.astype(BF16)], axis=0), 1, 1)
        return 0

    lax.fori_loop(0, nj, spec_step, 0)

    nt = HALF * TAB
    t3 = tacc[...].reshape(2 * HALF, 2 * TAB, 2 * cf)

    def get(x, y, z):
        return t3[x * HALF : (x + 1) * HALF, y * TAB : (y + 1) * TAB, z * cf : (z + 1) * cf].reshape(nt, cf)

    ccc, ccs, csc, css = get(0, 0, 0), get(0, 0, 1), get(0, 1, 0), get(0, 1, 1)
    scc, scs, ssc, sss = get(1, 0, 0), get(1, 0, 1), get(1, 1, 0), get(1, 1, 1)
    pairs, power = [], jnp.zeros((1, cf), F32)
    for v, (b, c) in enumerate(((1, 1), (1, -1), (-1, 1), (-1, -1))):
        cosf = ccc - b * ssc - c * scs - (b * c) * css
        sinf = scc + b * csc + c * ccs - (b * c) * sss
        hits = gacc[v * nt : (v + 1) * nt, 2 * cf : 3 * cf]
        power = power + jnp.sum(hits * (cosf * cosf + sinf * sinf), axis=0, keepdims=True)
        pairs.append((b, c, cosf, sinf))
    for i in range(3):
        power = power + pltpu.roll(power, fp << i, 1)
    kvec = nj * kloc
    scale = lax.rsqrt(power / (2 * kvec) + EPS) * (1.0 / kvec**0.5)
    grid = [jnp.zeros((nt, cf), F32)] * 8
    for v, (b, c, cosf, sinf) in enumerate(pairs):
        g = (gacc[v * nt : (v + 1) * nt, 0:cf] + gacc[v * nt : (v + 1) * nt, cf : 2 * cf]) * scale
        fc, fsn = g * cosf, g * sinf
        signs = (1, c, b, -b * c, 1, -c, -b, -b * c)
        picks = (fc, fsn, fsn, fc, fsn, fc, fc, fsn)
        grid = [old + s * x for old, s, x in zip(grid, signs, picks)]
    g3 = [x.reshape(HALF, TAB, cf) for x in grid]
    plane = [jnp.concatenate([g3[2 * i], g3[2 * i + 1]], axis=2) for i in range(4)]
    half = [jnp.concatenate([plane[2 * i], plane[2 * i + 1]], axis=1) for i in range(2)]
    tt = split(jnp.concatenate(half, axis=0).reshape(2 * HALF * 2 * TAB, 2 * cf).T)

    def inv_step(t, _):
        q = chunk(nq - 1 - t)
        field = mm3(tt, (xyh[q], xyl[q]))
        total = jnp.zeros((fp, ch), F32)
        for c in range(2 * TAB):
            if c % TAB < HALF and c != TAB:
                total = total + ztab[q, c : c + 1, :] * field[c * fp : (c + 1) * fp]
        for i in range(GROUP):
            p = q * GROUP + i
            lng[p] = total[0:fpd, i * BLOCK : (i + 1) * BLOCK]

            @pl.when(p != me)
            def _():
                back_copy(p, me).start()

        return 0

    lax.fori_loop(0, nq, inv_step, 0)
    back[pl.ds(me, 1)] = lng[pl.ds(me, 1)]

    @pl.when(me > 0)
    def _():
        halo_copy(0).wait_recv()

    @pl.when(me + 1 < n)
    def _():
        halo_copy(1).wait_recv()

    put_window(0, split(halo[0]))
    put_window(2, split(halo[1]))

    acc[...] = jnp.zeros((width, rows), F32)
    spacing = REACH / (radial - 1)
    centers = lax.broadcasted_iota(jnp.int32, (radial, rows), 0).astype(F32) * spacing
    row_id = lax.broadcasted_iota(jnp.int32, (span, rows), 0)
    slots = slot_ref.shape[0]
    count = count_ref[...]

    def short_step(t, _):
        parts = []
        for u in range(SLOTS):
            s = t * SLOTS + u
            one = jnp.where(row_id == slot_ref[pl.ds(s, 1), :], 1.0, 0.0).astype(BF16)
            bh, bl = split(jnp.exp(-jnp.square((dist_ref[pl.ds(s, 1), :] - centers) / spacing)))
            parts.append(jnp.concatenate(
                [one, bh, bl, bh, jnp.zeros((BLOCK - 3 * radial, rows), BF16)], axis=0))
        pre = dot(wt[...], jnp.concatenate(parts, axis=1))
        total = acc[...]
        for u in range(SLOTS):
            h = pre[:, u * rows : (u + 1) * rows] + selft[...]
            live = count > t * SLOTS + u
            total = total + jnp.where(live, h + h * jnp.tanh(h), 0.0)
        acc[...] = total
        return 0

    lax.fori_loop(0, slots // SLOTS, short_step, 0)
    short = mm3(split((acc[...] * (1.0 / slots)).T), (wide[0, 0], wide[0, 1]))
    out_ref[...] = feat_ref[...] + short


    def wait_back(t, _):
        p = lax.rem(me + t, n)
        back_copy(p, p).wait_recv()
        return 0

    lax.fori_loop(1, n, wait_back, 0)
    for p in range(n):
        lt[p * fpd : (p + 1) * fpd, :] = back[p]
    total = out_ref[...] + lt[...].T
    normed = total * lax.rsqrt(jnp.mean(total * total, axis=1, keepdims=True) + EPS) * gain_ref[...]
    up = mm3(split(normed), (wide[1, 0], wide[1, 1]))
    h = 0.5 * up
    out_ref[...] = total + mm3(split(h + h * jnp.tanh(h)), (wide[2, 0], wide[2, 1]))

    def wait_sent(t, _):
        p = lax.rem(me + t, n)
        feat_copy(p, me).wait_send()
        back_copy(p, me).wait_send()
        return 0

    lax.fori_loop(1, n, wait_sent, 0)

    for k in range(1, nw):
        for copy in along_copies(lax.rem(iw + k, nw), iw):
            copy.wait_send()

    def wait_plane_sent(t, _):
        plane_copy(lax.rem(here + t, nr), here).wait_send()
        return 0

    lax.fori_loop(1, nr, wait_plane_sent, 0)
    for k in range(1, ng):
        core_copy(lax.rem(ig + k, ng), ig).wait_send()

    def wait_spec_sent(t, _):
        spec_copy(lax.rem(mine + t, nj), mine).wait_send()
        return 0

    lax.fori_loop(1, nj, wait_spec_sent, 0)

    @pl.when(me + 1 < n)
    def _():
        halo_copy(0).wait_send()

    @pl.when(me > 0)
    def _():
        halo_copy(1).wait_send()


def local(
    sizes, features, positions, wavevectors, neighbour_slots, neighbour_count, pair_distance,
    w_self, w_neighbour, w_edge, w_message, spec_filter, norm_gain, w_up, w_down,
):
    nb, nw, ng = sizes
    n, nj = nb * nw * ng, nw * ng
    rows, width = features.shape
    kloc = spec_filter.shape[0]
    fpd = width // n
    fp = max(fpd, 16)
    cf = TAB * fp
    ch = GROUP * BLOCK
    nq = n // GROUP
    nxy = 2 * HALF * 2 * TAB
    cols = nj * fpd
    if cols % 128:
        spec_filter = lax.dynamic_slice_in_dim(spec_filter, lax.axis_index("bead") * cols, cols, 1)
    vmem = pl.BlockSpec(memory_space=pltpu.VMEM)
    dma = pltpu.SemaphoreType.DMA
    return pl.pallas_call(
        functools.partial(body, sizes),
        out_shape=jax.ShapeDtypeStruct((rows, width), F32),
        in_specs=[vmem] * 8 + [pl.BlockSpec(memory_space=pl.ANY)] * 6,
        out_specs=vmem,
        scratch_shapes=[
            pltpu.VMEM((n, fpd, BLOCK), F32),
            pltpu.VMEM((n, fpd, BLOCK), F32),
            pltpu.VMEM((nj, fpd, kloc), F32),
            pltpu.VMEM((nj, fpd, kloc), F32),
            pltpu.VMEM((nb, ng, nw, 8, BLOCK), F32),
            pltpu.VMEM((ng, nw, 3, kloc), jnp.int32),
            pltpu.VMEM((2, rows, width), F32),
            pltpu.VMEM((nq, nxy, ch), BF16),
            pltpu.VMEM((nq, nxy, ch), BF16),
            pltpu.VMEM((nq, 2 * TAB, ch), F32),
            pltpu.VMEM((2 * TAB, ch), F32),
            pltpu.VMEM((2 * cf, ch), BF16),
            pltpu.VMEM((2 * cf, ch), BF16),
            pltpu.VMEM((nxy, 2 * cf), F32),
            pltpu.VMEM((n, fpd, BLOCK), F32),
            pltpu.VMEM((n, fpd, BLOCK), F32),
            pltpu.VMEM((width, rows), F32),
            pltpu.VMEM((width, 4 * BLOCK), BF16),
            pltpu.VMEM((width, rows), F32),
            pltpu.VMEM((width, rows), F32),
            pltpu.VMEM((4 * HALF * TAB, 3 * cf), F32),
            pltpu.VMEM((kloc, cols), F32),
            pltpu.VMEM((5, width, width), F32),
            pltpu.VMEM((3, 2, width, width), BF16),
            dma((n,)), dma((n,)), dma((nj,)), dma((nj,)), dma((2,)), dma((2,)), dma((n,)), dma((n,)),
            dma((nw,)), dma((nw,)), dma((nb * ng,)), dma((nb * ng,)), dma((nw,)), dma((nw,)), dma((ng,)), dma((ng,)), dma((6,)),
        ],
        compiler_params=pltpu.CompilerParams(
            collective_id=0, has_side_effects=True, vmem_limit_bytes=60 * 1024 * 1024),
        cost_estimate=pl.CostEstimate(flops=10**10, bytes_accessed=10**7, transcendentals=10**7),
    )(
        features, positions, wavevectors, neighbour_slots, neighbour_count[None], pair_distance,
        w_edge, norm_gain[None], spec_filter, w_self, w_neighbour, w_message, w_up, w_down,
    )


def solution(mesh):
    sizes = tuple(mesh.shape[a] for a in ("bead", "wave", "grp"))
    every = ("bead", "wave", "grp")
    placed = (
        P(every, None), P(None, every), P(None, ("wave", "grp")), P(None, every), P(every), P(None, every),
        P(), P(), P(), P(), P(("wave", "grp"), None), P(), P(), P(),
    )
    return jax.shard_map(
        functools.partial(local, sizes), mesh=mesh, in_specs=placed, out_specs=P(every, None), check_vma=False)
```

```python
import functools

import jax
import jax.numpy as jnp
from jax import lax
from jax.experimental import pallas as pl
from jax.experimental.pallas import tpu as pltpu
from jax.sharding import PartitionSpec as P

MESH = pl.DeviceIdType.MESH
F32, BF16 = jnp.float32, jnp.bfloat16
BLOCK = 128
TOP = 6
HALF = TOP + 1
TAB = 8
REACH = 2.5
EPS = 1e-05
TWO_PI = 6.283185307179586
GROUP = 4
SLOTS = 4


def split(x):
    hi = x.astype(BF16)
    return hi, (x - hi.astype(F32)).astype(BF16)


def dot(a, b, ca=1, cb=0):
    return lax.dot_general(a, b, (((ca,), (cb,)), ((), ())), preferred_element_type=F32)


def mm3(a, b, ca=1, cb=0):
    return dot(a[0], b[0], ca, cb) + (dot(a[0], b[1], ca, cb) + dot(a[1], b[0], ca, cb))


def body(
    sizes,
    feat_ref, pos_ref, wave_ref, slot_ref, count_ref, dist_ref, wedge_ref, gain_ref,
    spec_hbm, wself_hbm, wneigh_hbm, wmsg_hbm, wup_hbm, wdown_hbm,
    out_ref,
    pack, fall, spack, spall, tall, wall, halo, xyh, xyl, ztab, ytab, ah, al, tacc, lng, back, lt,
    wt, selft, acc, gacc, spec, weights, wide,
    fs, fr, ss, sr, hs, hr, bs, br, t1s, t1r, t2s, t2r, w1s, w1r, w2s, w2r, ls,
):
    nb, nw, ng = sizes
    n, nj = nb * nw * ng, nw * ng
    rows, width = feat_ref.shape
    fpd = width // n
    fp = max(fpd, 16)
    cf = TAB * fp
    ch = GROUP * BLOCK
    nq = n // GROUP
    kloc = spec_hbm.shape[0]
    cols = nj * fpd
    nr = nb * ng
    ib, iw, ig = lax.axis_index("bead"), lax.axis_index("wave"), lax.axis_index("grp")
    mine = iw * ng + ig
    me = ib * nj + mine

    def coords(p):
        return (lax.div(p, nj), lax.rem(lax.div(p, ng), nw), lax.rem(p, ng))

    at = ib * cols
    source = spec_hbm if cols % 128 else spec_hbm.at[:, pl.ds(pl.multiple_of(at, 128), cols)]
    fetch = [pltpu.make_async_copy(source, spec, ls.at[0])]
    for i, w in enumerate((wself_hbm, wneigh_hbm, wmsg_hbm, wup_hbm, wdown_hbm)):
        fetch.append(pltpu.make_async_copy(w, weights.at[i], ls.at[i + 1]))
    for copy in fetch:
        copy.start()

    barrier = pltpu.get_barrier_semaphore()

    def greet(t, _):
        pl.semaphore_signal(barrier, inc=1, device_id=coords(lax.rem(me + t, n)), device_id_type=MESH)
        return 0

    lax.fori_loop(1, n, greet, 0)

    ft = feat_ref[...].T
    angle = TWO_PI * pos_ref[...]
    trig = jnp.concatenate([jnp.cos(angle), jnp.sin(angle), jnp.zeros((2, rows), F32)], axis=0)
    tall[ib, ig, iw] = trig
    wall[ig, iw] = wave_ref[...]
    for p in range(n):
        pack[p] = ft[p * fpd : (p + 1) * fpd]
    pl.semaphore_wait(barrier, n - 1)

    def along_copies(w, slot):
        return [pltpu.make_async_remote_copy(
            src_ref=buf.at[ig, iw] if buf is wall else buf.at[ib, ig, iw],
            dst_ref=buf.at[ig, slot] if buf is wall else buf.at[ib, ig, slot],
            send_sem=send.at[w], recv_sem=recv.at[slot],
            device_id=(ib, w, ig), device_id_type=MESH) for buf, send, recv in ((tall, t1s, t1r), (wall, w1s, w1r))]

    def plane_copy(r, slot):
        b, g = lax.div(slot, ng), lax.rem(slot, ng)
        return pltpu.make_async_remote_copy(
            src_ref=tall.at[ib, ig], dst_ref=tall.at[b, g], send_sem=t2s.at[r], recv_sem=t2r.at[slot],
            device_id=(lax.div(r, ng), iw, lax.rem(r, ng)), device_id_type=MESH)

    def core_copy(g, slot):
        return pltpu.make_async_remote_copy(
            src_ref=wall.at[ig], dst_ref=wall.at[slot], send_sem=w2s.at[g], recv_sem=w2r.at[slot],
            device_id=(ib, iw, g), device_id_type=MESH)

    def feat_copy(p, slot):
        return pltpu.make_async_remote_copy(
            src_ref=pack.at[p], dst_ref=fall.at[slot], send_sem=fs.at[p], recv_sem=fr.at[slot],
            device_id=coords(p), device_id_type=MESH)

    def spec_copy(j, slot):
        return pltpu.make_async_remote_copy(
            src_ref=spack.at[j], dst_ref=spall.at[slot], send_sem=ss.at[j], recv_sem=sr.at[slot],
            device_id=coords(ib * nj + j), device_id_type=MESH)

    def halo_copy(side):
        p = me + 1 if side == 0 else me - 1
        return pltpu.make_async_remote_copy(
            src_ref=feat_ref, dst_ref=halo.at[side], send_sem=hs.at[side], recv_sem=hr.at[side],
            device_id=coords(p), device_id_type=MESH)

    def back_copy(p, slot):
        return pltpu.make_async_remote_copy(
            src_ref=lng.at[p], dst_ref=back.at[slot], send_sem=bs.at[p], recv_sem=br.at[slot],
            device_id=coords(p), device_id_type=MESH)

    for k in range(1, nw):
        for copy in along_copies(lax.rem(iw + k, nw), iw):
            copy.start()
    here = ib * ng + ig
    far = sorted(range(nw), key=lambda k: -min(k, nw - k))
    for k in far:
        w = lax.rem(iw + k, nw)

        def send_feat(t, _):
            r = lax.rem(here + t, nr)
            feat_copy((lax.div(r, ng) * nw + w) * ng + lax.rem(r, ng), me).start()
            return 0

        lax.fori_loop(0 if k else 1, nr, send_feat, 0)

    fetch[0].wait()
    st = spec[...].T
    for j in range(nj):
        spack[j] = st[j * fpd : (j + 1) * fpd]
    for k in range(1, nw):
        for copy in along_copies(iw, lax.rem(iw + k, nw)):
            copy.wait_recv()

    def send_plane(t, _):
        plane_copy(lax.rem(here + t, nr), here).start()
        return 0

    lax.fori_loop(1, nr, send_plane, 0)
    for k in range(1, ng):
        core_copy(lax.rem(ig + k, ng), ig).start()

    def send_spec(t, _):
        j = lax.rem(mine + nj // 2 + t, nj)

        @pl.when(j != mine)
        def _():
            spec_copy(j, mine).start()

        return 0

    lax.fori_loop(0, nj, send_spec, 0)
    fall[pl.ds(me, 1)] = pack[pl.ds(me, 1)]
    spall[pl.ds(mine, 1)] = spack[pl.ds(mine, 1)]

    @pl.when(me == 0)
    def _():
        halo[0] = jnp.zeros((rows, width), F32)

    @pl.when(me == n - 1)
    def _():
        halo[1] = jnp.zeros((rows, width), F32)

    fetch[1].wait()
    own = split(feat_ref[...])
    selft[...] = 0.5 * mm3(own, split(weights[0])).T
    fetch[2].wait()
    wn = split(weights[1])
    span = 3 * BLOCK

    def put_window(at, part):
        hi, lo = split(0.5 * mm3(part, wn).T)
        wt[:, at * BLOCK : (at + 1) * BLOCK] = hi
        wt[:, span + at * BLOCK : span + (at + 1) * BLOCK] = lo

    put_window(1, own)
    radial = wedge_ref.shape[0]
    eh, el = split(0.5 * wedge_ref[...].T)
    wt[:, 2 * span : 2 * span + BLOCK] = jnp.concatenate(
        [eh, eh, el, jnp.zeros((width, BLOCK - 3 * radial), BF16)], axis=1)

    for i in range(3):
        fetch[i + 3].wait()
        wide[i, 0], wide[i, 1] = split(weights[i + 2])

    tacc[...] = jnp.zeros(tacc.shape, F32)

    def wait_plane(t, _):
        r = lax.rem(here + t, nr)
        plane_copy(r, r).wait_recv()
        return 0

    lax.fori_loop(1, nr, wait_plane, 0)
    for k in range(1, ng):
        core_copy(ig, lax.rem(ig + k, ng)).wait_recv()
    per = nq // nb
    first = lax.div(mine, GROUP)

    def chunk(t):
        return lax.rem(ib + t, nb) * per + lax.rem(first + lax.div(t, nb), per)

    def fwd_step(t, _):
        q = chunk(t)

        @pl.when((t == nq // 2) & (me + 1 < n))
        def _():
            halo_copy(0).start()

        @pl.when((t == nq // 2) & (me > 0))
        def _():
            halo_copy(1).start()

        for i in range(GROUP):
            p = q * GROUP + i

            @pl.when(p != me)
            def _():
                feat_copy(p, p).wait_recv()

        blocks = [fall[q * GROUP + i] for i in range(GROUP)]
        f = jnp.concatenate(blocks, axis=1)
        if fp > fpd:
            f = jnp.concatenate([f, jnp.zeros((fp - fpd, ch), F32)], axis=0)
        places = [(lax.div(p, nj), lax.rem(p, ng), lax.rem(lax.div(p, ng), nw)) for p in [q * GROUP + i for i in range(GROUP)]]
        trigs = jnp.concatenate([tall[b, g, w] for b, g, w in places], axis=1)
        c1, s1 = trigs[0:3], trigs[3:6]
        cs, sn = [jnp.ones_like(c1), c1], [jnp.zeros_like(c1), s1]
        for a in range(2, HALF):
            cs.append(cs[-1] * c1 - sn[-1] * s1)
            sn.append(sn[-1] * c1 + cs[-2] * s1)
        zero = jnp.zeros((1, ch), F32)
        for a in range(HALF):
            ytab[a : a + 1, :] = cs[a][1:2]
            ytab[TAB + a : TAB + a + 1, :] = sn[a][1:2]
            ztab[q, a : a + 1, :] = cs[a][2:3]
            ztab[q, TAB + a : TAB + a + 1, :] = sn[a][2:3]
        for a in (HALF, TAB + HALF):
            ytab[a : a + 1, :] = zero
            ztab[q, a : a + 1, :] = zero
        yt = ytab[...]
        for a in range(2 * HALF):
            x = cs[a][0:1] if a < HALF else sn[a - HALF][0:1]
            hi, lo = split(x * yt)
            xyh[q, a * 2 * TAB : (a + 1) * 2 * TAB, :] = hi
            xyl[q, a * 2 * TAB : (a + 1) * 2 * TAB, :] = lo
        for c in range(2 * TAB):
            hi, lo = split(ztab[q, c : c + 1, :] * f)
            ah[c * fp : (c + 1) * fp, :] = hi
            al[c * fp : (c + 1) * fp, :] = lo
        tacc[...] += mm3((xyh[q], xyl[q]), (ah[...], al[...]), 1, 1)
        return 0

    lax.fori_loop(0, nq, fwd_step, 0)

    def wait_spec(t, _):
        j = lax.rem(mine + t, nj)
        spec_copy(j, j).wait_recv()
        return 0

    lax.fori_loop(1, nj, wait_spec, 0)
    nvec = 4 * HALF * TAB
    gacc[...] = jnp.zeros(gacc.shape, F32)

    def spec_step(j, _):
        sp = spall[j]
        if fp > fpd:
            sp = jnp.concatenate([sp, jnp.zeros((fp - fpd, kloc), F32)], axis=0)
        vec = wall[lax.rem(j, ng), lax.div(j, ng)].astype(F32)
        kx, ky, kz = (vec[i : i + 1] for i in range(3))
        flip = jnp.where(kx < 0, -1.0, 1.0)
        ky, kz = ky * flip, kz * flip
        kind = jnp.where(ky < 0, 2.0, 0.0) + jnp.where(kz < 0, 1.0, 0.0)
        at = kind * (HALF * TAB) + jnp.abs(kx) * TAB + jnp.abs(ky)
        vec_id = lax.broadcasted_iota(jnp.int32, (nvec, kloc), 0).astype(F32)
        pick = jnp.where(vec_id == at, 1.0, 0.0).astype(BF16)
        c = jnp.abs(kz)
        vals = jnp.concatenate([jnp.where(c == i, sp, 0.0) for i in range(TAB)], axis=0)
        hits = jnp.concatenate(
            [jnp.broadcast_to(jnp.where(c == i, 1.0, 0.0), (fp, kloc)) for i in range(TAB)], axis=0)
        vh, vl = split(vals)
        gacc[...] += dot(pick, jnp.concatenate([vh, vl, hits.astype(BF16)], axis=0), 1, 1)
        return 0

    lax.fori_loop(0, nj, spec_step, 0)

    nt = HALF * TAB
    t3 = tacc[...].reshape(2 * HALF, 2 * TAB, 2 * cf)

    def get(x, y, z):
        return t3[x * HALF : (x + 1) * HALF, y * TAB : (y + 1) * TAB, z * cf : (z + 1) * cf].reshape(nt, cf)

    ccc, ccs, csc, css = get(0, 0, 0), get(0, 0, 1), get(0, 1, 0), get(0, 1, 1)
    scc, scs, ssc, sss = get(1, 0, 0), get(1, 0, 1), get(1, 1, 0), get(1, 1, 1)
    pairs, power = [], jnp.zeros((1, cf), F32)
    for v, (b, c) in enumerate(((1, 1), (1, -1), (-1, 1), (-1, -1))):
        cosf = ccc - b * ssc - c * scs - (b * c) * css
        sinf = scc + b * csc + c * ccs - (b * c) * sss
        hits = gacc[v * nt : (v + 1) * nt, 2 * cf : 3 * cf]
        power = power + jnp.sum(hits * (cosf * cosf + sinf * sinf), axis=0, keepdims=True)
        pairs.append((b, c, cosf, sinf))
    for i in range(3):
        power = power + pltpu.roll(power, fp << i, 1)
    kvec = nj * kloc
    scale = lax.rsqrt(power / (2 * kvec) + EPS) * (1.0 / kvec**0.5)
    grid = [jnp.zeros((nt, cf), F32)] * 8
    for v, (b, c, cosf, sinf) in enumerate(pairs):
        g = (gacc[v * nt : (v + 1) * nt, 0:cf] + gacc[v * nt : (v + 1) * nt, cf : 2 * cf]) * scale
        fc, fsn = g * cosf, g * sinf
        signs = (1, c, b, -b * c, 1, -c, -b, -b * c)
        picks = (fc, fsn, fsn, fc, fsn, fc, fc, fsn)
        grid = [old + s * x for old, s, x in zip(grid, signs, picks)]
    g3 = [x.reshape(HALF, TAB, cf) for x in grid]
    plane = [jnp.concatenate([g3[2 * i], g3[2 * i + 1]], axis=2) for i in range(4)]
    half = [jnp.concatenate([plane[2 * i], plane[2 * i + 1]], axis=1) for i in range(2)]
    tt = split(jnp.concatenate(half, axis=0).reshape(2 * HALF * 2 * TAB, 2 * cf).T)

    def inv_step(t, _):
        q = chunk(nq - 1 - t)
        field = mm3(tt, (xyh[q], xyl[q]))
        total = jnp.zeros((fp, ch), F32)
        for c in range(2 * TAB):
            if c % TAB < HALF and c != TAB:
                total = total + ztab[q, c : c + 1, :] * field[c * fp : (c + 1) * fp]
        for i in range(GROUP):
            p = q * GROUP + i
            lng[p] = total[0:fpd, i * BLOCK : (i + 1) * BLOCK]

            @pl.when(p != me)
            def _():
                back_copy(p, me).start()

        return 0

    lax.fori_loop(0, nq, inv_step, 0)
    back[pl.ds(me, 1)] = lng[pl.ds(me, 1)]

    @pl.when(me > 0)
    def _():
        halo_copy(0).wait_recv()

    @pl.when(me + 1 < n)
    def _():
        halo_copy(1).wait_recv()

    put_window(0, split(halo[0]))
    put_window(2, split(halo[1]))

    acc[...] = jnp.zeros((width, rows), F32)
    spacing = REACH / (radial - 1)
    centers = lax.broadcasted_iota(jnp.int32, (radial, rows), 0).astype(F32) * spacing
    row_id = lax.broadcasted_iota(jnp.int32, (span, rows), 0)
    slots = slot_ref.shape[0]
    count = count_ref[...]

    def short_step(t, _):
        parts = []
        for u in range(SLOTS):
            s = t * SLOTS + u
            one = jnp.where(row_id == slot_ref[pl.ds(s, 1), :], 1.0, 0.0).astype(BF16)
            bh, bl = split(jnp.exp(-jnp.square((dist_ref[pl.ds(s, 1), :] - centers) / spacing)))
            parts.append(jnp.concatenate(
                [one, one, bh, bl, bh, jnp.zeros((BLOCK - 3 * radial, rows), BF16)], axis=0))
        pre = dot(wt[...], jnp.concatenate(parts, axis=1))
        total = acc[...]
        for u in range(SLOTS):
            h = pre[:, u * rows : (u + 1) * rows] + selft[...]
            live = count > t * SLOTS + u
            total = total + jnp.where(live, h + h * jnp.tanh(h), 0.0)
        acc[...] = total
        return 0

    lax.fori_loop(0, slots // SLOTS, short_step, 0)
    short = mm3(split((acc[...] * (1.0 / slots)).T), (wide[0, 0], wide[0, 1]))
    out_ref[...] = feat_ref[...] + short


    def wait_back(t, _):
        p = lax.rem(me + t, n)
        back_copy(p, p).wait_recv()
        return 0

    lax.fori_loop(1, n, wait_back, 0)
    for p in range(n):
        lt[p * fpd : (p + 1) * fpd, :] = back[p]
    total = out_ref[...] + lt[...].T
    normed = total * lax.rsqrt(jnp.mean(total * total, axis=1, keepdims=True) + EPS) * gain_ref[...]
    up = mm3(split(normed), (wide[1, 0], wide[1, 1]))
    h = 0.5 * up
    out_ref[...] = total + mm3(split(h + h * jnp.tanh(h)), (wide[2, 0], wide[2, 1]))

    def wait_sent(t, _):
        p = lax.rem(me + t, n)
        feat_copy(p, me).wait_send()
        back_copy(p, me).wait_send()
        return 0

    lax.fori_loop(1, n, wait_sent, 0)

    for k in range(1, nw):
        for copy in along_copies(lax.rem(iw + k, nw), iw):
            copy.wait_send()

    def wait_plane_sent(t, _):
        plane_copy(lax.rem(here + t, nr), here).wait_send()
        return 0

    lax.fori_loop(1, nr, wait_plane_sent, 0)
    for k in range(1, ng):
        core_copy(lax.rem(ig + k, ng), ig).wait_send()

    def wait_spec_sent(t, _):
        spec_copy(lax.rem(mine + t, nj), mine).wait_send()
        return 0

    lax.fori_loop(1, nj, wait_spec_sent, 0)

    @pl.when(me + 1 < n)
    def _():
        halo_copy(0).wait_send()

    @pl.when(me > 0)
    def _():
        halo_copy(1).wait_send()


def local(
    sizes, features, positions, wavevectors, neighbour_slots, neighbour_count, pair_distance,
    w_self, w_neighbour, w_edge, w_message, spec_filter, norm_gain, w_up, w_down,
):
    nb, nw, ng = sizes
    n, nj = nb * nw * ng, nw * ng
    rows, width = features.shape
    kloc = spec_filter.shape[0]
    fpd = width // n
    fp = max(fpd, 16)
    cf = TAB * fp
    ch = GROUP * BLOCK
    nq = n // GROUP
    nxy = 2 * HALF * 2 * TAB
    cols = nj * fpd
    if cols % 128:
        spec_filter = lax.dynamic_slice_in_dim(spec_filter, lax.axis_index("bead") * cols, cols, 1)
    vmem = pl.BlockSpec(memory_space=pltpu.VMEM)
    dma = pltpu.SemaphoreType.DMA
    return pl.pallas_call(
        functools.partial(body, sizes),
        out_shape=jax.ShapeDtypeStruct((rows, width), F32),
        in_specs=[vmem] * 8 + [pl.BlockSpec(memory_space=pl.ANY)] * 6,
        out_specs=vmem,
        scratch_shapes=[
            pltpu.VMEM((n, fpd, BLOCK), F32),
            pltpu.VMEM((n, fpd, BLOCK), F32),
            pltpu.VMEM((nj, fpd, kloc), F32),
            pltpu.VMEM((nj, fpd, kloc), F32),
            pltpu.VMEM((nb, ng, nw, 8, BLOCK), F32),
            pltpu.VMEM((ng, nw, 3, kloc), jnp.int32),
            pltpu.VMEM((2, rows, width), F32),
            pltpu.VMEM((nq, nxy, ch), BF16),
            pltpu.VMEM((nq, nxy, ch), BF16),
            pltpu.VMEM((nq, 2 * TAB, ch), F32),
            pltpu.VMEM((2 * TAB, ch), F32),
            pltpu.VMEM((2 * cf, ch), BF16),
            pltpu.VMEM((2 * cf, ch), BF16),
            pltpu.VMEM((nxy, 2 * cf), F32),
            pltpu.VMEM((n, fpd, BLOCK), F32),
            pltpu.VMEM((n, fpd, BLOCK), F32),
            pltpu.VMEM((width, rows), F32),
            pltpu.VMEM((width, 7 * BLOCK), BF16),
            pltpu.VMEM((width, rows), F32),
            pltpu.VMEM((width, rows), F32),
            pltpu.VMEM((4 * HALF * TAB, 3 * cf), F32),
            pltpu.VMEM((kloc, cols), F32),
            pltpu.VMEM((5, width, width), F32),
            pltpu.VMEM((3, 2, width, width), BF16),
            dma((n,)), dma((n,)), dma((nj,)), dma((nj,)), dma((2,)), dma((2,)), dma((n,)), dma((n,)),
            dma((nw,)), dma((nw,)), dma((nb * ng,)), dma((nb * ng,)), dma((nw,)), dma((nw,)), dma((ng,)), dma((ng,)), dma((6,)),
        ],
        compiler_params=pltpu.CompilerParams(
            collective_id=0, has_side_effects=True, vmem_limit_bytes=60 * 1024 * 1024),
        cost_estimate=pl.CostEstimate(flops=10**10, bytes_accessed=10**7, transcendentals=10**7),
    )(
        features, positions, wavevectors, neighbour_slots, neighbour_count[None], pair_distance,
        w_edge, norm_gain[None], spec_filter, w_self, w_neighbour, w_message, w_up, w_down,
    )


def solution(mesh):
    sizes = tuple(mesh.shape[a] for a in ("bead", "wave", "grp"))
    every = ("bead", "wave", "grp")
    placed = (
        P(every, None), P(None, every), P(None, ("wave", "grp")), P(None, every), P(every), P(None, every),
        P(), P(), P(), P(), P(("wave", "grp"), None), P(), P(), P(),
    )
    return jax.shard_map(
        functools.partial(local, sizes), mesh=mesh, in_specs=placed, out_specs=P(every, None), check_vma=False)
```
